32 devices in a mesh: chan: 16 (over z, x, core), inp: 2 (over y).
Axes of the slice: x: 2, y: 2, z: 4, core: 2. Of those that a mesh axis runs over, the one named last changes fastest.
Arguments:
- voltages: bfloat16 [512, 2, 65536], P('inp', None, 'chan'), may hold values from -64 to 64
Outputs:
- delays: float32 [512, 512, 2, 512], P('inp', 'chan')
The draws below stay inside these ranges and needn't reach their ends.
All inputs are finite; a program needn't handle non-finite values.
Results may differ from the reference program's by a relative error of at most 0.0053.
Values may be sent and summed in bfloat16 or wider, within the bound.
A program may use at most 192 MiB of HBM per device.

```python
import math
import jax
import jax.numpy as jnp
from jax import lax

NINP = 512
NCH = 512
NSPEC = 128
TIME = 65536
N_INP = 2


def draw_voltages(key, part):
    subkeys = jax.random.split(key, 6)
    input_gains = jnp.exp(jax.random.uniform(subkeys[0], (NINP,), jnp.float32, math.log(0.5), math.log(4.0)))
    noise_part = jax.random.normal(subkeys[1], (NINP, 2, TIME), jnp.float32)
    amplitude = jax.random.uniform(subkeys[5], (NINP,), jnp.float32, 0.1, 0.4)
    fir_taps = 0.5 * jax.random.normal(subkeys[2], (NINP, 3), jnp.float32)
    colored = noise_part
    for offset in range(3):
        colored = colored + fir_taps[:, offset, None, None] * jnp.roll(noise_part, offset + 1, axis=2)
    sky_signal = jax.random.normal(subkeys[3], (2, TIME), jnp.float32)
    shifts = jnp.stack([jnp.roll(sky_signal, offset, axis=1) for offset in range(8)])
    delay_steps = jax.random.randint(subkeys[4], (NINP,), 0, 8)
    onehot = (delay_steps[:, None] == jnp.arange(8)[None, :]).astype(jnp.float32)
    delayed = jnp.einsum('im,mpt->ipt', onehot, shifts)
    voltage_draw = input_gains[:, None, None] * (colored + amplitude[:, None, None] * delayed)
    return jnp.clip(voltage_draw, -64.0, 64.0).astype(jnp.bfloat16)


def setup_inputs(seed: int = 0) -> dict:
    keys = jax.random.split(jax.random.key(seed), 2)
    voltages = draw_voltages(jax.random.fold_in(keys[1], 71), 0)
    return dict(voltages=voltages)


def taper_weights(count):
    position = jnp.arange(count, dtype=jnp.float32)
    return 0.5 - 0.5 * jnp.cos(2.0 * math.pi * (position + 0.5) / count)

def channel_table(count):
    indices = jnp.arange(count, dtype=jnp.int32)
    product = indices[:, None] * indices[None, :] % count
    angle = 2.0 * math.pi / count * product.astype(jnp.float32)
    window = taper_weights(count)[:, None] / math.sqrt(count)
    cosine = window * jnp.cos(angle)
    sine = window * jnp.sin(angle)
    upper = jnp.concatenate([cosine, -sine], axis=1)
    lower = jnp.concatenate([sine, cosine], axis=1)
    return jnp.concatenate([upper, lower], axis=0).astype(jnp.bfloat16)

def round_half(values):
    narrow = lax.optimization_barrier(values.astype(jnp.bfloat16))
    return narrow.astype(jnp.float32)

def reference(voltages):
    block_rows = NINP // N_INP
    samples = voltages.reshape(NINP, 2, NSPEC, NCH).transpose(0, 2, 1, 3).reshape(NINP * NSPEC, 2 * NCH)
    spectra = jnp.dot(samples, channel_table(NCH), preferred_element_type=jnp.float32).astype(jnp.bfloat16)
    spectra = spectra.reshape(NINP, NSPEC, 2, NCH)
    stacked = spectra.transpose(3, 0, 2, 1).reshape(NCH, NINP, 2 * NSPEC).astype(jnp.float32)
    rotated = jnp.concatenate([-stacked[:, :, NSPEC:], stacked[:, :, :NSPEC]], axis=2)
    power = lax.optimization_barrier(jnp.sum(stacked * stacked, axis=2)) / NSPEC + 1e-06
    inverse_root = lax.rsqrt(power)
    taper = taper_weights(NCH)
    factor = math.sqrt(NSPEC / NCH)

    def one_block(block_index):
        start = (block_index * block_rows).astype(jnp.int32)
        rows = lax.dynamic_slice_in_dim(stacked, start, block_rows, 1)
        real_part = jnp.einsum('cit,cjt->cij', rows, stacked, precision=lax.Precision.HIGHEST)
        imag_part = jnp.einsum('cit,cjt->cij', rows, rotated, precision=lax.Precision.HIGHEST)
        row_scale = lax.dynamic_slice_in_dim(inverse_root, start, block_rows, 1)
        scaling = row_scale[:, :, None] * inverse_root[:, None, :] / NSPEC
        rho_real = round_half(real_part * scaling) * taper[:, None, None]
        rho_imag = round_half(imag_part * scaling) * taper[:, None, None]
        complex_vis = rho_real + 1j * rho_imag
        spectrum = jnp.fft.fft(complex_vis, axis=0) * factor
        result = jnp.stack([jnp.real(spectrum), jnp.imag(spectrum)], axis=0).transpose(2, 3, 0, 1)
        rows_global = start + jnp.arange(block_rows, dtype=jnp.int32)
        cols_global = jnp.arange(NINP, dtype=jnp.int32)
        same = rows_global[:, None] == cols_global[None, :]
        return jnp.where(same[:, :, None, None], jnp.zeros_like(result), result)
    blocks = lax.map(one_block, jnp.arange(N_INP, dtype=jnp.int32))
    return blocks.reshape(NINP, NINP, 2, NCH)
```

```python
import functools
import math

import jax
import jax.numpy as jnp
import ml_dtypes
import numpy as np
from jax import lax
from jax.experimental import pallas as pl
from jax.experimental.pallas import tpu as pltpu
from jax.sharding import PartitionSpec as P

NCH = 512
VMEM_LIMIT = 56 * 1024 * 1024


def taper_weights(count):
    position = np.arange(count, dtype=np.float64)
    return 0.5 - 0.5 * np.cos(2.0 * math.pi * (position + 0.5) / count)


def angles(count):
    indices = np.arange(count, dtype=np.int64)
    return 2.0 * math.pi / count * ((indices[:, None] * indices[None, :]) % count)


def channel_table_rows(count):
    angle = angles(count)
    window = taper_weights(count)[:, None] / math.sqrt(count)
    cosine = window * np.cos(angle)
    sine = window * np.sin(angle)
    upper = np.concatenate([cosine, -sine], axis=1)
    lower = np.concatenate([sine, cosine], axis=1)
    table = np.concatenate([upper, lower], axis=0).astype(np.float32)
    return np.ascontiguousarray(table.T).astype(ml_dtypes.bfloat16)


def delay_table(count, spec_total):
    angle = angles(count)
    window = taper_weights(count)[:, None] * math.sqrt(spec_total / count)
    cosine = window * np.cos(angle)
    sine = window * np.sin(angle)
    from_real = np.concatenate([cosine, -sine], axis=1)
    from_imag = np.concatenate([sine, cosine], axis=1)
    return np.stack([from_real, from_imag], axis=1).astype(ml_dtypes.bfloat16)


def channelize(voltages):
    rows, _, local_time = voltages.shape
    spec_local = local_time // NCH
    turned = voltages.transpose(1, 0, 2)
    table = jnp.asarray(channel_table_rows(NCH))
    lines = NCH * 2 * spec_local
    pieces = rows // 128 if rows % 128 == 0 else 1
    width = rows // pieces
    call = pl.pallas_call(
        functools.partial(channelize_kernel, spec_local),
        grid=(pieces, spec_local),
        in_specs=[
            pl.BlockSpec((2 * NCH, 2 * NCH), lambda r, s: (0, 0)),
            pl.BlockSpec((2, width, NCH), lambda r, s: (0, r, s)),
        ],
        out_specs=pl.BlockSpec((lines, width), lambda r, s: (0, r)),
        out_shape=jax.ShapeDtypeStruct((lines, rows), jnp.bfloat16),
        scratch_shapes=[pltpu.VMEM((lines, width), jnp.float32)],
        compiler_params=pltpu.CompilerParams(vmem_limit_bytes=VMEM_LIMIT),
    )
    return call(table, turned)


def channelize_kernel(spec_local, table_ref, volt_ref, out_ref, held):
    step = pl.program_id(1)
    last = (((1,), (1,)), ((), ()))
    depth = 2 * spec_local
    for part in range(2):
        rows = pl.ds(part * NCH, NCH)
        result = lax.dot_general(
            table_ref[rows, :NCH], volt_ref[0], last, preferred_element_type=jnp.float32
        ) + lax.dot_general(
            table_ref[rows, NCH:], volt_ref[1], last, preferred_element_type=jnp.float32
        )
        held[pl.ds(part * spec_local + step, NCH, stride=depth), :] = result

    @pl.when(step == spec_local - 1)
    def _():
        out_ref[...] = held[...].astype(jnp.bfloat16)


def visibility_kernel(spec_total, count, half_depth, mine_ref, piece_ref, out_ref, held):
    step = pl.program_id(1)
    sources, _, depth, rows = mine_ref.shape
    mine = mine_ref[:, 0]
    turned = jnp.concatenate([mine[:, half_depth:], -mine[:, :half_depth]], axis=1)
    mine = mine.reshape(sources * depth, rows)
    turned = turned.reshape(sources * depth, rows)
    piece = piece_ref[0, :, 0].reshape(sources * depth, rows)

    def scale(block):
        wide = block.astype(jnp.float32)
        power = jnp.sum(wide * wide, axis=0, keepdims=True) / spec_total + 1e-06
        return lax.rsqrt(power)

    own = scale(mine) / spec_total
    other = jnp.transpose(jnp.broadcast_to(scale(piece), (8, rows)))[:, :1]
    numbers = (((0,), (0,)), ((), ()))
    for part, block in enumerate((mine, turned)):
        value = lax.dot_general(piece, block, numbers, preferred_element_type=jnp.float32)
        value = value * (other * own)
        cols = value.shape[1]
        for start in range(0, cols, min(128, cols)):
            wide = min(128, cols)
            held[part * (cols // wide) + start // wide, pl.ds(step, rows, stride=count), :] = value[
                :, start : start + wide
            ]

    @pl.when(step == count - 1)
    def _():
        wide = held.shape[2]
        for tile in range(held.shape[0]):
            out_ref[:, tile * wide : (tile + 1) * wide] = held[tile].astype(jnp.bfloat16)


def visibilities(mine, gathered, spec_total):
    inputs = gathered.shape[0]
    sources, count, depth, rows = mine.shape
    wide = min(128, rows)
    call = pl.pallas_call(
        functools.partial(visibility_kernel, spec_total, count, depth // 2),
        grid=(inputs, count),
        in_specs=[
            pl.BlockSpec((sources, 1, depth, rows), lambda h, c: (0, c, 0, 0)),
            pl.BlockSpec((1, sources, 1, depth, rows), lambda h, c: (h, 0, c, 0, 0)),
        ],
        out_specs=pl.BlockSpec((rows * count, 2 * rows), lambda h, c: (h, 0)),
        out_shape=jax.ShapeDtypeStruct((inputs * rows * count, 2 * rows), jnp.bfloat16),
        scratch_shapes=[pltpu.VMEM((2 * rows // wide, rows * count, wide), jnp.float32)],
        compiler_params=pltpu.CompilerParams(vmem_limit_bytes=VMEM_LIMIT),
    )
    return call(mine, gathered)


def delay_kernel(chunks, rows, offset_ref, table_ref, *refs):
    blocks, out_ref = refs[:chunks], refs[chunks]
    numbers = (((0,), (0,)), ((), ()))
    total = None
    for chunk in range(chunks):
        sources, _, count, wide = blocks[chunk].shape
        block = blocks[chunk][:, 0].reshape(sources * count, wide)
        for part in range(2):
            term = lax.dot_general(
                block[:, part * rows : (part + 1) * rows],
                table_ref[chunk, part],
                numbers,
                preferred_element_type=jnp.float32,
            )
            total = term if total is None else total + term
    column = offset_ref[0] + pl.program_id(0)
    same = lax.broadcasted_iota(jnp.int32, (rows, 1), 0) == column
    total = jnp.where(same, 0.0, total)
    for part in range(2):
        out_ref[:, 0, part, :] = total[:, part * NCH : (part + 1) * NCH]


def delay_spectra(received, table, offset, rows):
    chunks = len(received)
    sources, cols, count, wide = received[0].shape
    call = pl.pallas_call(
        functools.partial(delay_kernel, chunks, rows),
        grid=(cols,),
        in_specs=[
            pl.BlockSpec(memory_space=pltpu.SMEM),
            pl.BlockSpec(table.shape, lambda j: (0, 0, 0, 0)),
        ]
        + [pl.BlockSpec((sources, 1, count, wide), lambda j: (0, j, 0, 0))] * chunks,
        out_specs=pl.BlockSpec((rows, 1, 2, NCH), lambda j: (0, j, 0, 0)),
        out_shape=jax.ShapeDtypeStruct((rows, cols, 2, NCH), jnp.float32),
        compiler_params=pltpu.CompilerParams(vmem_limit_bytes=VMEM_LIMIT),
    )
    return call(offset, table, *received)


def shards(voltages):
    rows, _, local_time = voltages.shape
    chan_count = lax.axis_size("chan")
    inp_count = lax.axis_size("inp")
    spec_local = local_time // NCH
    spec_total = spec_local * chan_count
    chan_local = NCH // chan_count
    col_local = rows * inp_count // chan_count
    depth = 2 * spec_local
    count = chan_local // 2 if chan_local % 32 == 0 else chan_local
    chunks = chan_local // count

    spectra = channelize(voltages).reshape(chan_count, chunks, count, depth, rows)
    mine = []
    for chunk in range(chunks):
        mine.append(lax.all_to_all(spectra[:, chunk], "chan", split_axis=0, concat_axis=0, tiled=True))
    received = []
    for chunk in range(chunks):
        gathered = lax.all_gather(mine[chunk], "inp", axis=0, tiled=False)
        rho = visibilities(mine[chunk], gathered, spec_total)
        rho = rho.reshape(chan_count, col_local, count, 2 * rows)
        received.append(lax.all_to_all(rho, "chan", split_axis=0, concat_axis=0, tiled=True))

    table = delay_table(NCH, spec_total)
    table = table.reshape(chan_count, chunks, count, 2, 2 * NCH).transpose(1, 3, 0, 2, 4)
    table = jnp.asarray(np.ascontiguousarray(table).reshape(chunks, 2, chan_count * count, 2 * NCH))
    offset = lax.axis_index("chan") * col_local - lax.axis_index("inp") * rows
    return delay_spectra(received, table, offset.astype(jnp.int32).reshape(1), rows)


def solution(mesh):
    in_specs = (P("inp", None, "chan"),)
    out_specs = P("inp", "chan", None, None)
    return jax.shard_map(shards, mesh=mesh, in_specs=in_specs, out_specs=out_specs, check_vma=False)
```

```python
import functools
import math

import jax
import jax.numpy as jnp
import ml_dtypes
import numpy as np
from jax import lax
from jax.experimental import pallas as pl
from jax.experimental.pallas import tpu as pltpu
from jax.sharding import PartitionSpec as P

NCH = 512
VMEM_LIMIT = 56 * 1024 * 1024


def taper_weights(count):
    position = np.arange(count, dtype=np.float64)
    return 0.5 - 0.5 * np.cos(2.0 * math.pi * (position + 0.5) / count)


def angles(count):
    indices = np.arange(count, dtype=np.int64)
    return 2.0 * math.pi / count * ((indices[:, None] * indices[None, :]) % count)


def channel_table_rows(count):
    angle = angles(count)
    window = taper_weights(count)[:, None] / math.sqrt(count)
    cosine = window * np.cos(angle)
    sine = window * np.sin(angle)
    upper = np.concatenate([cosine, -sine], axis=1)
    lower = np.concatenate([sine, cosine], axis=1)
    table = np.concatenate([upper, lower], axis=0).astype(np.float32)
    return np.ascontiguousarray(table.T).astype(ml_dtypes.bfloat16)


def delay_table(count, spec_total):
    angle = angles(count)
    window = taper_weights(count)[:, None] * math.sqrt(spec_total / count)
    cosine = window * np.cos(angle)
    sine = window * np.sin(angle)
    from_real = np.concatenate([cosine, -sine], axis=1)
    from_imag = np.concatenate([sine, cosine], axis=1)
    return np.stack([from_real, from_imag], axis=1).astype(ml_dtypes.bfloat16)


def channelize(voltages):
    rows, _, local_time = voltages.shape
    spec_local = local_time // NCH
    turned = voltages.transpose(1, 0, 2)
    table = jnp.asarray(channel_table_rows(NCH))
    lines = NCH * 2 * spec_local
    pieces = rows // 128 if rows % 128 == 0 else 1
    width = rows // pieces
    call = pl.pallas_call(
        functools.partial(channelize_kernel, spec_local),
        grid=(pieces, spec_local),
        in_specs=[
            pl.BlockSpec((2 * NCH, 2 * NCH), lambda r, s: (0, 0)),
            pl.BlockSpec((2, width, NCH), lambda r, s: (0, r, s)),
        ],
        out_specs=pl.BlockSpec((lines, width), lambda r, s: (0, r)),
        out_shape=jax.ShapeDtypeStruct((lines, rows), jnp.bfloat16),
        scratch_shapes=[pltpu.VMEM((lines, width), jnp.float32)],
        compiler_params=pltpu.CompilerParams(vmem_limit_bytes=VMEM_LIMIT),
    )
    return call(table, turned)


def channelize_kernel(spec_local, table_ref, volt_ref, out_ref, held):
    step = pl.program_id(1)
    last = (((1,), (1,)), ((), ()))
    depth = 2 * spec_local
    for part in range(2):
        rows = pl.ds(part * NCH, NCH)
        result = lax.dot_general(
            table_ref[rows, :NCH], volt_ref[0], last, preferred_element_type=jnp.float32
        ) + lax.dot_general(
            table_ref[rows, NCH:], volt_ref[1], last, preferred_element_type=jnp.float32
        )
        held[pl.ds(part * spec_local + step, NCH, stride=depth), :] = result

    @pl.when(step == spec_local - 1)
    def _():
        out_ref[...] = held[...].astype(jnp.bfloat16)


def visibility_kernel(spec_total, count, half_depth, mine_ref, piece_ref, out_ref, held):
    step = pl.program_id(1)
    sources, _, depth, rows = mine_ref.shape
    mine = mine_ref[:, 0]
    turned = jnp.concatenate([mine[:, half_depth:], -mine[:, :half_depth]], axis=1)
    mine = mine.reshape(sources * depth, rows)
    turned = turned.reshape(sources * depth, rows)
    piece = piece_ref[0, :, 0].reshape(sources * depth, rows)

    def scale(block):
        wide = block.astype(jnp.float32)
        power = jnp.sum(wide * wide, axis=0, keepdims=True) / spec_total + 1e-06
        return lax.rsqrt(power)

    own = scale(mine) / spec_total
    other = jnp.transpose(jnp.broadcast_to(scale(piece), (8, rows)))[:, :1]
    numbers = (((0,), (0,)), ((), ()))
    for part, block in enumerate((mine, turned)):
        value = lax.dot_general(piece, block, numbers, preferred_element_type=jnp.float32)
        value = value * (other * own)
        cols = value.shape[1]
        for start in range(0, cols, min(128, cols)):
            wide = min(128, cols)
            held[part * (cols // wide) + start // wide, pl.ds(step, rows, stride=count), :] = value[
                :, start : start + wide
            ]

    @pl.when(step == count - 1)
    def _():
        wide = held.shape[2]
        for tile in range(held.shape[0]):
            out_ref[:, tile * wide : (tile + 1) * wide] = held[tile].astype(jnp.bfloat16)


def visibilities(mine, gathered, spec_total):
    inputs = gathered.shape[0]
    sources, count, depth, rows = mine.shape
    wide = min(128, rows)
    call = pl.pallas_call(
        functools.partial(visibility_kernel, spec_total, count, depth // 2),
        grid=(inputs, count),
        in_specs=[
            pl.BlockSpec((sources, 1, depth, rows), lambda h, c: (0, c, 0, 0)),
            pl.BlockSpec((1, sources, 1, depth, rows), lambda h, c: (h, 0, c, 0, 0)),
        ],
        out_specs=pl.BlockSpec((rows * count, 2 * rows), lambda h, c: (h, 0)),
        out_shape=jax.ShapeDtypeStruct((inputs * rows * count, 2 * rows), jnp.bfloat16),
        scratch_shapes=[pltpu.VMEM((2 * rows // wide, rows * count, wide), jnp.float32)],
        compiler_params=pltpu.CompilerParams(vmem_limit_bytes=VMEM_LIMIT),
    )
    return call(mine, gathered)


def delay_kernel(chunks, rows, offset_ref, table_ref, *refs):
    blocks, out_ref = refs[:chunks], refs[chunks]
    numbers = (((0,), (0,)), ((), ()))
    total = None
    for chunk in range(chunks):
        sources, _, count, wide = blocks[chunk].shape
        block = blocks[chunk][:, 0].reshape(sources * count, wide)
        for part in range(2):
            term = lax.dot_general(
                block[:, part * rows : (part + 1) * rows],
                table_ref[chunk, part],
                numbers,
                preferred_element_type=jnp.float32,
            )
            total = term if total is None else total + term
    column = offset_ref[0] + pl.program_id(0)
    same = lax.broadcasted_iota(jnp.int32, (rows, 1), 0) == column
    total = jnp.where(same, 0.0, total)
    for part in range(2):
        out_ref[:, 0, part, :] = total[:, part * NCH : (part + 1) * NCH]


def delay_spectra(received, table, offset, rows):
    sources, chunks, cols, count, wide = received.shape
    call = pl.pallas_call(
        functools.partial(delay_kernel, chunks, rows),
        grid=(cols,),
        in_specs=[
            pl.BlockSpec(memory_space=pltpu.SMEM),
            pl.BlockSpec(table.shape, lambda j: (0, 0, 0, 0)),
        ]
        + [
            pl.BlockSpec((sources, None, 1, count, wide), lambda j, chunk=chunk: (0, chunk, j, 0, 0))
            for chunk in range(chunks)
        ],
        out_specs=pl.BlockSpec((rows, 1, 2, NCH), lambda j: (0, j, 0, 0)),
        out_shape=jax.ShapeDtypeStruct((rows, cols, 2, NCH), jnp.float32),
        compiler_params=pltpu.CompilerParams(vmem_limit_bytes=VMEM_LIMIT),
    )
    return call(offset, table, *([received] * chunks))


def shards(voltages):
    rows, _, local_time = voltages.shape
    chan_count = lax.axis_size("chan")
    inp_count = lax.axis_size("inp")
    spec_local = local_time // NCH
    spec_total = spec_local * chan_count
    chan_local = NCH // chan_count
    col_local = rows * inp_count // chan_count
    depth = 2 * spec_local
    count = chan_local // 2 if chan_local % 32 == 0 else chan_local
    chunks = chan_local // count

    spectra = channelize(voltages).reshape(chan_count, chunks, count, depth, rows)
    mine = []
    for chunk in range(chunks):
        mine.append(lax.all_to_all(spectra[:, chunk], "chan", split_axis=0, concat_axis=0, tiled=True))
    rhos = []
    for chunk in range(chunks):
        gathered = lax.all_gather(mine[chunk], "inp", axis=0, tiled=False)
        rho = visibilities(mine[chunk], gathered, spec_total)
        rhos.append(rho.reshape(chan_count, col_local, count, 2 * rows))
    rho = jnp.stack(rhos, axis=1)
    received = lax.all_to_all(rho, "chan", split_axis=0, concat_axis=0, tiled=True)

    table = delay_table(NCH, spec_total)
    table = table.reshape(chan_count, chunks, count, 2, 2 * NCH).transpose(1, 3, 0, 2, 4)
    table = jnp.asarray(np.ascontiguousarray(table).reshape(chunks, 2, chan_count * count, 2 * NCH))
    offset = lax.axis_index("chan") * col_local - lax.axis_index("inp") * rows
    return delay_spectra(received, table, offset.astype(jnp.int32).reshape(1), rows)


def solution(mesh):
    in_specs = (P("inp", None, "chan"),)
    out_specs = P("inp", "chan", None, None)
    return jax.shard_map(shards, mesh=mesh, in_specs=in_specs, out_specs=out_specs, check_vma=False)
```
